32 devices in a mesh: rows: 16 (over z, y, x), cols: 2 (over core).
Axes of the slice: x: 2, y: 2, z: 4, core: 2. Of those that a mesh axis runs over, the one named last changes fastest.
Arguments:
- descriptors: bfloat16 [16384, 512], P('rows'), may hold values from -17 to 17, as said below
- sparse_points: bfloat16 [2048, 512], P('cols'), may hold values from -0.25 to 0.25
Outputs:
- q_factor: float32 [16384, 256], P('rows')
- r_rows: float32 [256, 2048], P(None, 'cols')
- trailing: bfloat16 [16384, 2048], P('rows', 'cols')
The draws below stay inside these ranges and needn't reach their ends.
Inputs may be any that keep to these rules, and one draw needn't show every extreme that they name: `descriptors`: each row is a random vector times a positive scale of its own.
All inputs are finite; a program needn't handle non-finite values.
Results may differ from the reference program's by a relative error of at most 0.001.
Values may be sent and summed in bfloat16 or wider, within the bound.
A program may use at most 64 MiB of HBM per device.

```python
import math
import jax
import jax.numpy as jnp
from jax import lax

DW = 512
COL_DEV = 1024
PANEL = 128
NROWS = 16384
SPARSE = 2048


def draw_descriptors(key, part):
    key_values = jax.random.fold_in(key, 11)
    key_scales = jax.random.fold_in(key, 23)
    position = jnp.arange(NROWS, dtype=jnp.float32) / NROWS
    rising = ((1.0 + 2.0 * position) ** 0.25)[:, None]
    values = jax.random.truncated_normal(key_values, -4.0, 4.0, (NROWS, DW), jnp.float32)
    spread = jnp.exp(0.5 * jax.random.uniform(key_scales, (NROWS, 1), jnp.float32, 0.0, math.log(10.0)))
    return (values * spread * rising).astype(jnp.bfloat16)


def steps_of(stream_key, shape, split, least, top_value):
    gain, own = 1.0, jax.random.fold_in(stream_key, 6)
    for axis_at, parts in split:
        steps = jnp.exp(jax.random.uniform(jax.random.fold_in(own, axis_at), (parts,), jnp.float32, least / len(split), top_value / len(split)))
        gain = gain * jnp.repeat(steps, shape[axis_at] // parts).reshape([-1 if axis == axis_at else 1 for axis in range(len(shape))])
    return gain


def gaussian(rng, extent, scale, reach, shards=(), kind=jnp.bfloat16):
    result = jax.random.normal(rng, extent, jnp.float32) * scale
    if len(shards) > 0:
        result = steps_of(rng, extent, shards, -0.22, 0.18) * result
    return jnp.clip(result, min=-reach, max=reach).astype(kind)


def setup_inputs(seed: int = 0) -> dict:
    streams_of = jax.random.split(jax.random.key(seed), 3)
    return {
        "descriptors": draw_descriptors(jax.random.fold_in(streams_of[2], 71), 0),
        "sparse_points": gaussian(streams_of[1], (SPARSE, DW), DW ** -0.5, 0.25, ((0, 2),)),
    }


HIGHEST_PRECISION = lax.Precision.HIGHEST

def factor_panel(panel):
    gram_matrix = jnp.dot(panel.T.astype(jnp.float32), panel.astype(jnp.float32), precision=HIGHEST_PRECISION, preferred_element_type=jnp.float32) / NROWS
    lower = jnp.linalg.cholesky(gram_matrix)
    q_transposed = lax.linalg.triangular_solve(lower, panel.T, left_side=True, lower=True)
    return q_transposed.T

def reference(descriptors, sparse_points):
    inner_dots = jnp.dot(descriptors.astype(jnp.float32), sparse_points.T.astype(jnp.float32), preferred_element_type=jnp.float32)
    kernel = inner_dots * inner_dots
    q_one = factor_panel(kernel[:, :PANEL])
    r_one = jnp.dot(q_one.T.astype(jnp.float32), kernel.astype(jnp.float32), precision=HIGHEST_PRECISION, preferred_element_type=jnp.float32) / NROWS
    updated = kernel - jnp.dot(q_one.astype(jnp.float32), r_one.astype(jnp.float32), precision=HIGHEST_PRECISION, preferred_element_type=jnp.float32)
    q_two = factor_panel(updated[:, COL_DEV:COL_DEV + PANEL])
    r_two = jnp.dot(q_two.T.astype(jnp.float32), updated.astype(jnp.float32), precision=HIGHEST_PRECISION, preferred_element_type=jnp.float32) / NROWS
    trailing = updated - jnp.dot(q_two.astype(jnp.float32), r_two.astype(jnp.float32), precision=HIGHEST_PRECISION, preferred_element_type=jnp.float32)
    q_factor = jnp.concatenate([q_one, q_two], axis=1)
    r_rows = jnp.concatenate([r_one, r_two], axis=0)
    return (q_factor, r_rows, trailing.astype(jnp.bfloat16))
```

```python
import functools

import jax
import jax.numpy as jnp
from jax import lax
from jax.experimental import pallas as pl
from jax.experimental.pallas import tpu as pltpu
from jax.sharding import PartitionSpec as P

PANEL = 128
BLOCK = 32
LANES = 128
HIGHEST = lax.Precision.HIGHEST
F32 = jnp.float32
BF16 = jnp.bfloat16
MESH = pl.DeviceIdType.MESH


def dot_nt(a, b, precision=None):
    return lax.dot_general(
        a, b, (((1,), (1,)), ((), ())), precision=precision, preferred_element_type=F32
    )


def dot_nn(a, b, precision=None):
    return lax.dot_general(
        a, b, (((1,), (0,)), ((), ())), precision=precision, preferred_element_type=F32
    )


def dot_tn(a, b, precision=None):
    return lax.dot_general(
        a, b, (((0,), (0,)), ((), ())), precision=precision, preferred_element_type=F32
    )


def split(value):
    high = value.astype(BF16)
    return high, (value - high.astype(F32)).astype(BF16)


def three_pass(a_high, a_low, b_high, b_low):
    return dot_nn(a_high, b_high) + (dot_nn(a_high, b_low) + dot_nn(a_low, b_high))


def factor_block(work, at):
    tile_at, off = at // LANES * LANES, at % LANES
    tile = work[at : at + BLOCK, tile_at : tile_at + LANES]
    row = lax.broadcasted_iota(jnp.int32, (BLOCK, LANES), 0)
    lane = lax.broadcasted_iota(jnp.int32, (BLOCK, LANES), 1)
    rows = lax.broadcasted_iota(jnp.int32, (BLOCK, 1), 0)
    inverse = jnp.where(row == lane, 1.0, 0.0).astype(F32)
    for j in range(BLOCK - 1):
        column = tile[:, off + j : off + j + 1]
        pivot = tile[j : j + 1, off + j : off + j + 1]
        factor = jnp.where(rows > j, column / pivot, 0.0)
        tile = tile - factor * tile[j : j + 1, :]
        inverse = inverse - factor * inverse[j : j + 1, :]
    pivots = jnp.sum(jnp.where(lane == row + off, tile, 0.0), axis=1, keepdims=True)
    return (inverse * lax.rsqrt(pivots))[:, :BLOCK]


def factor_step(work, at):
    size = work.shape[0]
    panel = dot_nn(factor_block(work, at), work[at : at + BLOCK, :], HIGHEST)
    work[at : at + BLOCK, :] = panel
    rest = at + BLOCK
    if rest < size:
        start = rest // LANES * LANES
        change = dot_tn(panel[:, start:size], panel, HIGHEST)
        work[rest:size, :] = work[rest:size, :] - change[rest - start :, :]


def reduce_kernel(
    n_rows, n_cols, inner, total_rows,
    d_ref, p_ref, pp_ref, s_ref, linv_ref,
    pp, k_high, k_low, part, full, recv_one, recv_two, gram_one, gram_two, gram_own, gram, work,
    pp_send, pp_recv, sends, recvs, grams_send, grams_recv, swap_send, swap_recv, out_sem,
):
    outer = n_rows // inner
    me_row, me_col = lax.axis_index("rows"), lax.axis_index("cols")
    me_in, me_out = lax.rem(me_row, inner), lax.div(me_row, inner)
    joint = 2 * PANEL
    blocks = part.shape[0] // joint

    def inner_peer(t):
        at = lax.rem(me_in + t, inner)
        return at, (me_out * inner + at, me_col)

    def outer_peer(t):
        at = lax.rem(me_out + t, outer)
        return at, (at * inner + me_in, me_col)

    barrier = pltpu.get_barrier_semaphore()
    for t in range(1, inner):
        pl.semaphore_signal(barrier, inc=1, device_id=inner_peer(t)[1], device_id_type=MESH)
    for t in range(1, outer):
        pl.semaphore_signal(barrier, inc=1, device_id=outer_peer(t)[1], device_id_type=MESH)
    for t in range(1, n_cols):
        to = lax.rem(me_col + t, n_cols)
        pl.semaphore_signal(barrier, inc=1, device_id=(me_row, to), device_id_type=MESH)
    pl.semaphore_wait(barrier, inner + outer + n_cols - 3)

    def share(source, target_of, send_sem, recv_sem, own):
        def copy(which, t):
            to = lax.rem(which + t, n_cols)
            return pltpu.make_async_remote_copy(
                src_ref=source, dst_ref=target_of(which),
                send_sem=send_sem.at[which, t - 1], recv_sem=recv_sem.at[which],
                device_id=(me_row, to), device_id_type=MESH,
            )

        def start():
            for which in range(2):
                @pl.when(me_col == which)
                def _():
                    for t in range(1, n_cols):
                        copy(which, t).start()
                    own(which)

        def finish():
            for which in range(2):
                @pl.when(me_col != which)
                def _():
                    copy(which, 1).wait_recv()

        def drain():
            for which in range(2):
                @pl.when(me_col == which)
                def _():
                    for t in range(1, n_cols):
                        copy(which, t).wait_send()

        return start, finish, drain

    def own_points(which):
        pp[which * PANEL : (which + 1) * PANEL, :] = p_ref[:PANEL, :]

    points_start, points_finish, points_drain = share(
        p_ref.at[pl.ds(0, PANEL)],
        lambda which: pp.at[pl.ds(which * PANEL, PANEL)],
        pp_send, pp_recv, own_points,
    )
    points_start()
    for block in range(blocks // 2):
        cols = slice(block * joint, (block + 1) * joint)
        dots = dot_nt(d_ref[...], p_ref[cols, :])
        k_high[:, cols], k_low[:, cols] = split(dots * dots)
    points_finish()
    dots = dot_nt(pp[...], d_ref[...])
    j_high, j_low = split(dots * dots)
    pp_ref[...] = pp[...]

    def products(block):
        cols = slice(block * joint, (block + 1) * joint)
        value = three_pass(j_high, j_low, k_high[:, cols], k_low[:, cols])
        part[block * 2 * joint : block * 2 * joint + joint, :] = value[:, :PANEL]
        part[block * 2 * joint + joint : (block + 1) * 2 * joint, :] = value[:, PANEL:]

    piece = joint // inner

    def gram_scatter(t):
        to, device = inner_peer(t)
        return pltpu.make_async_remote_copy(
            src_ref=part.at[pl.ds(pl.multiple_of(to * piece, 8), piece)],
            dst_ref=gram_one.at[t - 1],
            send_sem=grams_send.at[0, t - 1], recv_sem=grams_recv.at[0, t - 1],
            device_id=device, device_id_type=MESH,
        )

    def gram_exchange(t):
        device = outer_peer(t)[1]
        return pltpu.make_async_remote_copy(
            src_ref=gram_two.at[me_out], dst_ref=gram_two.at[me_out],
            send_sem=grams_send.at[1, t - 1], recv_sem=grams_recv.at[1, t - 1],
            device_id=device, device_id_type=MESH,
        )

    own_piece = pl.ds(pl.multiple_of(me_in * piece, 8), piece)

    def gram_gather(t):
        device = inner_peer(t)[1]
        return pltpu.make_async_remote_copy(
            src_ref=gram_own.at[own_piece], dst_ref=gram_own.at[own_piece],
            send_sem=grams_send.at[2, t - 1], recv_sem=grams_recv.at[2, t - 1],
            device_id=device, device_id_type=MESH,
        )

    products(0)
    for t in range(1, inner):
        gram_scatter(t).start()
    for block in range(1, blocks // 2):
        products(block)

    first = joint if (part.shape[0] - joint) % (16 * n_rows) == 0 else 0
    chunk = (part.shape[0] - first) // 2
    wide, narrow = chunk // inner, chunk // n_rows

    def bulk(c):
        base = first + c * chunk

        def wide_at(i):
            return pl.ds(pl.multiple_of(base + i * wide, 8), wide)

        def narrow_at(o):
            return pl.ds(pl.multiple_of(base + me_in * wide + o * narrow, 8), narrow)

        def copy(stage, t):
            to, device = (inner_peer if stage in (0, 3) else outer_peer)(t)
            source, target = (
                (lambda: (part.at[wide_at(to)], recv_one.at[c, t - 1])),
                (lambda: (part.at[narrow_at(to)], recv_two.at[c, t - 1])),
                (lambda: (full.at[narrow_at(me_out)],) * 2),
                (lambda: (full.at[wide_at(me_in)],) * 2),
            )[stage]()
            return pltpu.make_async_remote_copy(
                src_ref=source, dst_ref=target,
                send_sem=sends.at[c, stage, t - 1], recv_sem=recvs.at[c, stage, t - 1],
                device_id=device, device_id_type=MESH,
            )

        def copies(stage):
            return [copy(stage, t) for t in range(1, inner if stage in (0, 3) else outer)]

        def start(stage):
            for one in copies(stage):
                one.start()

        def step(stage):
            for one in copies(stage):
                one.wait_recv()
            if stage == 0:
                for one in copies(stage):
                    one.wait_send()
                value = part[wide_at(me_in), :]
                for t in range(inner - 1):
                    value = value + recv_one[c, t]
                part[wide_at(me_in), :] = value
            if stage == 1:
                value = part[narrow_at(me_out), :]
                for t in range(outer - 1):
                    value = value + recv_two[c, t]
                full[narrow_at(me_out), :] = value
            if stage < 3:
                start(stage + 1)

        def drain():
            for stage in range(1, 4):
                for one in copies(stage):
                    one.wait_send()

        return start, step, drain

    (start_a, step_a, drain_a), (start_b, step_b, drain_b) = bulk(0), bulk(1)

    for t in range(1, inner):
        gram_scatter(t).wait_recv()
    value = part[own_piece, :]
    for t in range(inner - 1):
        value = value + gram_one[t]
    gram_two[me_out] = value
    for t in range(1, outer):
        gram_exchange(t).start()
    for t in range(1, inner):
        gram_scatter(t).wait_send()
    start_a(0)
    for t in range(1, outer):
        gram_exchange(t).wait_recv()
    value = gram_two[0]
    for o in range(1, outer):
        value = value + gram_two[o]
    gram_own[own_piece, :] = value
    for t in range(1, inner):
        gram_gather(t).start()
    start_b(0)
    for t in range(1, inner):
        gram_gather(t).wait_recv()

    def own_gram(which):
        gram[which] = gram_own[...]

    gram_start, gram_finish, gram_drain = share(
        gram_own, lambda which: gram.at[which], swap_send, swap_recv, own_gram
    )
    gram_start()
    gram_finish()
    work[:, :PANEL] = gram[0] / total_rows
    work[:, PANEL:joint] = gram[1] / total_rows
    row = lax.broadcasted_iota(jnp.int32, (joint, joint), 0)
    lane = lax.broadcasted_iota(jnp.int32, (joint, joint), 1)
    work[:, joint:] = jnp.where(row == lane, 1.0, 0.0).astype(F32)

    pending = [
        functools.partial(step, stage) for stage in range(4) for step in (step_a, step_b)
    ]
    for at in range(0, joint, BLOCK):
        factor_step(work, at)
        if pending and at >= BLOCK:
            pending.pop(0)()
    linv_ref[...] = work[:, joint:]
    for step in pending:
        step()
    rest = pl.ds(first, part.shape[0] - first)
    results = [pltpu.make_async_copy(full.at[rest], s_ref.at[rest], out_sem.at[0])]
    if first > 0:
        head = s_ref.at[pl.ds(0, joint)]
        results.append(pltpu.make_async_copy(gram_own, head, out_sem.at[1]))
    for result in results:
        result.start()
    points_drain()
    gram_drain()
    for t in range(1, outer):
        gram_exchange(t).wait_send()
    for t in range(1, inner):
        gram_gather(t).wait_send()
    drain_a()
    drain_b()
    for result in results:
        result.wait()


def reduced(descriptors, points, n_rows, n_cols):
    rows, width = descriptors.shape
    cols = points.shape[0]
    joint = 2 * PANEL
    inner = 4 if n_rows % 4 == 0 else 1
    outer = n_rows // inner
    flat = cols // PANEL * joint
    first = joint if (flat - joint) % (16 * n_rows) == 0 else 0
    chunk = (flat - first) // 2
    most = max(inner, outer, 2) - 1
    vmem = pl.BlockSpec(memory_space=pltpu.VMEM)
    dma = pltpu.SemaphoreType.DMA
    return pl.pallas_call(
        functools.partial(reduce_kernel, n_rows, n_cols, inner, float(rows * n_rows)),
        out_shape=(
            jax.ShapeDtypeStruct((joint, width), BF16),
            jax.ShapeDtypeStruct((flat, PANEL), F32),
            jax.ShapeDtypeStruct((joint, joint), F32),
        ),
        in_specs=[vmem, vmem],
        out_specs=(vmem, pl.BlockSpec(memory_space=pl.ANY), vmem),
        scratch_shapes=[
            pltpu.VMEM((joint, width), BF16),
            pltpu.VMEM((rows, cols), BF16),
            pltpu.VMEM((rows, cols), BF16),
            pltpu.VMEM((flat, PANEL), F32),
            pltpu.VMEM((flat, PANEL), F32),
            pltpu.VMEM((2, inner - 1, chunk // inner, PANEL), F32),
            pltpu.VMEM((2, outer - 1, chunk // n_rows, PANEL), F32),
            pltpu.VMEM((inner - 1, joint // inner, PANEL), F32),
            pltpu.VMEM((outer, joint // inner, PANEL), F32),
            pltpu.VMEM((joint, PANEL), F32),
            pltpu.VMEM((2, joint, PANEL), F32),
            pltpu.VMEM((joint, 2 * joint), F32),
            dma((2, n_cols - 1)),
            dma((2,)),
            dma((2, 4, most)),
            dma((2, 4, most)),
            dma((3, most)),
            dma((3, most)),
            dma((2, n_cols - 1)),
            dma((2,)),
            dma((2,)),
        ],
        compiler_params=pltpu.CompilerParams(
            collective_id=0, has_side_effects=True, vmem_limit_bytes=40 * 1024 * 1024
        ),
        name="gram_and_products",
    )(descriptors, points)


def finish_kernel(
    total_rows, d_ref, p_ref, pp_ref, s_ref, linv_ref, q_ref, r_ref, t_ref, r_high, r_low
):
    joint = 2 * PANEL

    @pl.when(pl.program_id(0) == 0)
    def _():
        for block in range(r_ref.shape[1] // PANEL):
            cols = slice(block * PANEL, (block + 1) * PANEL)
            sums = s_ref[block * joint : (block + 1) * joint, :]
            value = dot_nn(linv_ref[...], sums, HIGHEST) / total_rows
            r_ref[:, cols] = value
            r_high[:, cols], r_low[:, cols] = split(value)

    dots = dot_nt(d_ref[...], pp_ref[...])
    q = dot_nt(dots * dots, linv_ref[...], HIGHEST)
    q_ref[...] = q
    q_high, q_low = split(q)
    for block in range(r_ref.shape[1] // joint):
        cols = slice(block * joint, (block + 1) * joint)
        dots = dot_nt(d_ref[...], p_ref[cols, :])
        change = three_pass(q_high, q_low, r_high[:, cols], r_low[:, cols])
        t_ref[:, cols] = (dots * dots - change).astype(BF16)


def finished(descriptors, points, panel_points, sums, inverse, total_rows):
    rows, width = descriptors.shape
    cols = points.shape[0]
    joint = 2 * PANEL
    tile = 256
    whole = lambda shape: pl.BlockSpec(shape, lambda i: (0, 0))
    tiled = lambda lanes: pl.BlockSpec((tile, lanes), lambda i: (i, 0))
    return pl.pallas_call(
        functools.partial(finish_kernel, total_rows),
        out_shape=(
            jax.ShapeDtypeStruct((rows, joint), F32),
            jax.ShapeDtypeStruct((joint, cols), F32),
            jax.ShapeDtypeStruct((rows, cols), BF16),
        ),
        grid=(rows // tile,),
        in_specs=[
            tiled(width),
            whole((cols, width)),
            whole((joint, width)),
            whole(sums.shape),
            whole((joint, joint)),
        ],
        out_specs=(tiled(joint), whole((joint, cols)), tiled(cols)),
        scratch_shapes=[pltpu.VMEM((joint, cols), BF16), pltpu.VMEM((joint, cols), BF16)],
        compiler_params=pltpu.CompilerParams(vmem_limit_bytes=40 * 1024 * 1024),
        name="factors_and_remainder",
    )(descriptors, points, panel_points, sums, inverse)


def solution(mesh):
    n_rows, n_cols = mesh.shape["rows"], mesh.shape["cols"]

    def on_device(descriptors, sparse_points):
        panel_points, sums, inverse = reduced(descriptors, sparse_points, n_rows, n_cols)
        total_rows = float(descriptors.shape[0] * n_rows)
        return finished(descriptors, sparse_points, panel_points, sums, inverse, total_rows)

    in_specs = (P("rows", None), P("cols", None))
    out_specs = (P("rows", None), P(None, "cols"), P("rows", "cols"))
    return jax.shard_map(
        on_device, mesh=mesh, in_specs=in_specs, out_specs=out_specs, check_vma=False
    )
```

```python
import functools

import jax
import jax.numpy as jnp
from jax import lax
from jax.experimental import pallas as pl
from jax.experimental.pallas import tpu as pltpu
from jax.sharding import PartitionSpec as P

PANEL = 128
BLOCK = 32
SUB = 8
LANES = 128
HIGHEST = lax.Precision.HIGHEST
F32 = jnp.float32
BF16 = jnp.bfloat16
MESH = pl.DeviceIdType.MESH


def dot_nt(a, b, precision=None):
    return lax.dot_general(
        a, b, (((1,), (1,)), ((), ())), precision=precision, preferred_element_type=F32
    )


def dot_nn(a, b, precision=None):
    return lax.dot_general(
        a, b, (((1,), (0,)), ((), ())), precision=precision, preferred_element_type=F32
    )


def dot_tn(a, b, precision=None):
    return lax.dot_general(
        a, b, (((0,), (0,)), ((), ())), precision=precision, preferred_element_type=F32
    )


def split(value):
    high = value.astype(BF16)
    return high, (value - high.astype(F32)).astype(BF16)


def three_pass(a_high, a_low, b_high, b_low):
    return dot_nn(a_high, b_high) + (dot_nn(a_high, b_low) + dot_nn(a_low, b_high))


def factor_block(tile, off):
    row = lax.broadcasted_iota(jnp.int32, (BLOCK, LANES), 0)
    lane = lax.broadcasted_iota(jnp.int32, (BLOCK, LANES), 1)
    inverse = jnp.where(row == lane, 1.0, 0.0).astype(F32)
    done = []
    for top in range(0, BLOCK, SUB):
        left = BLOCK - top
        rows = row[:left, :]
        columns = [
            jnp.broadcast_to(tile[:, off + top + j : off + top + j + 1], (left, LANES))
            for j in range(SUB)
        ]
        scale = jnp.ones((SUB, LANES), F32)
        for j in range(SUB):
            pivot = columns[j][j : j + 1, :]
            factor = jnp.where(rows > j, columns[j] * (1.0 / pivot), 0.0)
            for k in range(j + 1, SUB):
                columns[k] = columns[k] - factor * columns[k][j : j + 1, :]
            tile = tile - factor * tile[j : j + 1, :]
            inverse = inverse - factor * inverse[j : j + 1, :]
            scale = jnp.where(rows[:SUB] == j, lax.rsqrt(pivot), scale)
        done.append(inverse[:SUB] * scale)
        tile, inverse = tile[SUB:], inverse[SUB:]
    return jnp.concatenate(done, axis=0)[:, :BLOCK]


def factor_step(work, at):
    size = work.shape[0]
    tile_at = at // LANES * LANES
    rest = at + BLOCK
    start = min(rest // LANES * LANES, size)
    stop = size + -(-rest // LANES) * LANES
    factor = factor_block(work[at:rest, tile_at : tile_at + LANES], at - tile_at)
    panel = dot_nn(factor, work[at:rest, start:stop], HIGHEST)
    work[at:rest, start:stop] = panel
    if rest < size:
        turned = panel[:, : size - start].T
        for low, high in ((rest, rest + BLOCK), (rest + BLOCK, size)):
            if low < high:
                change = dot_nn(turned[low - start : high - start, :], panel, HIGHEST)
                work[low:high, start:stop] = work[low:high, start:stop] - change


def reduce_kernel(
    n_rows, n_cols, inner, total_rows,
    d_hbm, p_hbm, pp_ref, s_ref, linv_ref,
    d_ref, p_ref, pp, k_high, k_low, part, full, recv_one, recv_two, gram_one, gram_two, gram_own, gram, work,
    pp_send, pp_recv, sends, recvs, grams_send, grams_recv, swap_send, swap_recv, out_sem, in_sem,
):
    outer = n_rows // inner
    me_row, me_col = lax.axis_index("rows"), lax.axis_index("cols")
    me_in, me_out = lax.rem(me_row, inner), lax.div(me_row, inner)
    joint = 2 * PANEL
    blocks = part.shape[0] // joint

    def inner_peer(t):
        at = lax.rem(me_in + t, inner)
        return at, (me_out * inner + at, me_col)

    def outer_peer(t):
        at = lax.rem(me_out + t, outer)
        return at, (at * inner + me_in, me_col)

    barrier = pltpu.get_barrier_semaphore()
    for t in range(1, inner):
        pl.semaphore_signal(barrier, inc=1, device_id=inner_peer(t)[1], device_id_type=MESH)
    for t in range(1, outer):
        pl.semaphore_signal(barrier, inc=1, device_id=outer_peer(t)[1], device_id_type=MESH)
    for t in range(1, n_cols):
        to = lax.rem(me_col + t, n_cols)
        pl.semaphore_signal(barrier, inc=1, device_id=(me_row, to), device_id_type=MESH)
    load_d = pltpu.make_async_copy(d_hbm, d_ref, in_sem.at[0])
    load_p = pltpu.make_async_copy(p_hbm, p_ref, in_sem.at[1])
    load_p.start()
    load_d.start()
    pl.semaphore_wait(barrier, inner + outer + n_cols - 3)

    def share(source, target_of, send_sem, recv_sem, own):
        def copy(which, t):
            to = lax.rem(which + t, n_cols)
            return pltpu.make_async_remote_copy(
                src_ref=source, dst_ref=target_of(which),
                send_sem=send_sem.at[which, t - 1], recv_sem=recv_sem.at[which],
                device_id=(me_row, to), device_id_type=MESH,
            )

        def start():
            for which in range(2):
                @pl.when(me_col == which)
                def _():
                    for t in range(1, n_cols):
                        copy(which, t).start()

        def finish():
            for which in range(2):
                @pl.when(me_col == which)
                def _():
                    own(which)

                @pl.when(me_col != which)
                def _():
                    copy(which, 1).wait_recv()

        def drain():
            for which in range(2):
                @pl.when(me_col == which)
                def _():
                    for t in range(1, n_cols):
                        copy(which, t).wait_send()

        return start, finish, drain

    def own_points(which):
        pp[which * PANEL : (which + 1) * PANEL, :] = p_ref[:PANEL, :]

    points_start, points_finish, points_drain = share(
        p_hbm.at[pl.ds(0, PANEL)],
        lambda which: pp.at[pl.ds(which * PANEL, PANEL)],
        pp_send, pp_recv, own_points,
    )
    points_start()
    load_p.wait()
    load_d.wait()
    for block in range(blocks // 2):
        cols = slice(block * joint, (block + 1) * joint)
        dots = dot_nt(d_ref[...], p_ref[cols, :])
        k_high[:, cols], k_low[:, cols] = split(dots * dots)
    points_finish()
    dots = dot_nt(pp[...], d_ref[...])
    j_high, j_low = split(dots * dots)
    pp_ref[...] = pp[...]

    def products(block):
        cols = slice(block * joint, (block + 1) * joint)
        value = three_pass(j_high, j_low, k_high[:, cols], k_low[:, cols])
        part[block * 2 * joint : block * 2 * joint + joint, :] = value[:, :PANEL]
        part[block * 2 * joint + joint : (block + 1) * 2 * joint, :] = value[:, PANEL:]

    piece = joint // inner

    def gram_scatter(t):
        to, device = inner_peer(t)
        return pltpu.make_async_remote_copy(
            src_ref=part.at[pl.ds(pl.multiple_of(to * piece, 8), piece)],
            dst_ref=gram_one.at[t - 1],
            send_sem=grams_send.at[0, t - 1], recv_sem=grams_recv.at[0, t - 1],
            device_id=device, device_id_type=MESH,
        )

    def gram_exchange(t):
        device = outer_peer(t)[1]
        return pltpu.make_async_remote_copy(
            src_ref=gram_two.at[me_out], dst_ref=gram_two.at[me_out],
            send_sem=grams_send.at[1, t - 1], recv_sem=grams_recv.at[1, t - 1],
            device_id=device, device_id_type=MESH,
        )

    own_piece = pl.ds(pl.multiple_of(me_in * piece, 8), piece)

    def gram_gather(t):
        device = inner_peer(t)[1]
        return pltpu.make_async_remote_copy(
            src_ref=gram_own.at[own_piece], dst_ref=gram_own.at[own_piece],
            send_sem=grams_send.at[2, t - 1], recv_sem=grams_recv.at[2, t - 1],
            device_id=device, device_id_type=MESH,
        )

    products(0)
    for t in range(1, inner):
        gram_scatter(t).start()
    for block in range(1, blocks // 2):
        products(block)

    first = joint if (part.shape[0] - joint) % (16 * n_rows) == 0 else 0
    chunk = (part.shape[0] - first) // 2
    wide, narrow = chunk // inner, chunk // n_rows

    def bulk(c):
        base = first + c * chunk

        def wide_at(i):
            return pl.ds(pl.multiple_of(base + i * wide, 8), wide)

        def narrow_at(o):
            return pl.ds(pl.multiple_of(base + me_in * wide + o * narrow, 8), narrow)

        def copy(stage, t):
            to, device = (inner_peer if stage in (0, 3) else outer_peer)(t)
            source, target = (
                (lambda: (part.at[wide_at(to)], recv_one.at[c, t - 1])),
                (lambda: (part.at[narrow_at(to)], recv_two.at[c, t - 1])),
                (lambda: (full.at[narrow_at(me_out)],) * 2),
                (lambda: (full.at[wide_at(me_in)],) * 2),
            )[stage]()
            return pltpu.make_async_remote_copy(
                src_ref=source, dst_ref=target,
                send_sem=sends.at[c, stage, t - 1], recv_sem=recvs.at[c, stage, t - 1],
                device_id=device, device_id_type=MESH,
            )

        def copies(stage):
            return [copy(stage, t) for t in range(1, inner if stage in (0, 3) else outer)]

        def start(stage):
            for one in copies(stage):
                one.start()

        def step(stage):
            for one in copies(stage):
                one.wait_recv()
            if stage == 0:
                for one in copies(stage):
                    one.wait_send()
                value = part[wide_at(me_in), :]
                for t in range(inner - 1):
                    value = value + recv_one[c, t]
                part[wide_at(me_in), :] = value
            if stage == 1:
                value = part[narrow_at(me_out), :]
                for t in range(outer - 1):
                    value = value + recv_two[c, t]
                full[narrow_at(me_out), :] = value
            if stage < 3:
                start(stage + 1)

        def drain():
            for stage in range(1, 4):
                for one in copies(stage):
                    one.wait_send()

        return start, step, drain

    (start_a, step_a, drain_a), (start_b, step_b, drain_b) = bulk(0), bulk(1)

    for t in range(1, inner):
        gram_scatter(t).wait_recv()
    value = part[own_piece, :]
    for t in range(inner - 1):
        value = value + gram_one[t]
    gram_two[me_out] = value
    for t in range(1, outer):
        gram_exchange(t).start()
    for t in range(1, inner):
        gram_scatter(t).wait_send()
    start_a(0)
    for t in range(1, outer):
        gram_exchange(t).wait_recv()
    value = gram_two[0]
    for o in range(1, outer):
        value = value + gram_two[o]
    gram_own[own_piece, :] = value
    for t in range(1, inner):
        gram_gather(t).start()
    start_b(0)
    for t in range(1, inner):
        gram_gather(t).wait_recv()

    def own_gram(which):
        gram[which] = gram_own[...]

    gram_start, gram_finish, gram_drain = share(
        gram_own, lambda which: gram.at[which], swap_send, swap_recv, own_gram
    )
    gram_start()
    gram_finish()
    work[:, :PANEL] = gram[0] / total_rows
    work[:, PANEL:joint] = gram[1] / total_rows
    row = lax.broadcasted_iota(jnp.int32, (joint, joint), 0)
    lane = lax.broadcasted_iota(jnp.int32, (joint, joint), 1)
    work[:, joint:] = jnp.where(row == lane, 1.0, 0.0).astype(F32)

    pending = [
        functools.partial(step, stage) for stage in range(4) for step in (step_a, step_b)
    ]
    for at in range(0, joint, BLOCK):
        factor_step(work, at)
        if pending and at >= BLOCK:
            pending.pop(0)()
    linv_ref[...] = work[:, joint:]
    for step in pending:
        step()
    rest = pl.ds(first, part.shape[0] - first)
    results = [pltpu.make_async_copy(full.at[rest], s_ref.at[rest], out_sem.at[0])]
    if first > 0:
        head = s_ref.at[pl.ds(0, joint)]
        results.append(pltpu.make_async_copy(gram_own, head, out_sem.at[1]))
    for result in results:
        result.start()
    points_drain()
    gram_drain()
    for t in range(1, outer):
        gram_exchange(t).wait_send()
    for t in range(1, inner):
        gram_gather(t).wait_send()
    drain_a()
    drain_b()
    for result in results:
        result.wait()


def reduced(descriptors, points, n_rows, n_cols):
    rows, width = descriptors.shape
    cols = points.shape[0]
    joint = 2 * PANEL
    inner = 4 if n_rows % 4 == 0 else 1
    outer = n_rows // inner
    flat = cols // PANEL * joint
    first = joint if (flat - joint) % (16 * n_rows) == 0 else 0
    chunk = (flat - first) // 2
    most = max(inner, outer, 2) - 1
    vmem = pl.BlockSpec(memory_space=pltpu.VMEM)
    dma = pltpu.SemaphoreType.DMA
    return pl.pallas_call(
        functools.partial(reduce_kernel, n_rows, n_cols, inner, float(rows * n_rows)),
        out_shape=(
            jax.ShapeDtypeStruct((joint, width), BF16),
            jax.ShapeDtypeStruct((flat, PANEL), F32),
            jax.ShapeDtypeStruct((joint, joint), F32),
        ),
        in_specs=[pl.BlockSpec(memory_space=pltpu.HBM)] * 2,
        out_specs=(vmem, pl.BlockSpec(memory_space=pl.ANY), vmem),
        scratch_shapes=[
            pltpu.VMEM((rows, width), BF16),
            pltpu.VMEM((cols, width), BF16),
            pltpu.VMEM((joint, width), BF16),
            pltpu.VMEM((rows, cols), BF16),
            pltpu.VMEM((rows, cols), BF16),
            pltpu.VMEM((flat, PANEL), F32),
            pltpu.VMEM((flat, PANEL), F32),
            pltpu.VMEM((2, inner - 1, chunk // inner, PANEL), F32),
            pltpu.VMEM((2, outer - 1, chunk // n_rows, PANEL), F32),
            pltpu.VMEM((inner - 1, joint // inner, PANEL), F32),
            pltpu.VMEM((outer, joint // inner, PANEL), F32),
            pltpu.VMEM((joint, PANEL), F32),
            pltpu.VMEM((2, joint, PANEL), F32),
            pltpu.VMEM((joint, 2 * joint), F32),
            dma((2, n_cols - 1)),
            dma((2,)),
            dma((2, 4, most)),
            dma((2, 4, most)),
            dma((3, most)),
            dma((3, most)),
            dma((2, n_cols - 1)),
            dma((2,)),
            dma((2,)),
            dma((2,)),
        ],
        compiler_params=pltpu.CompilerParams(
            collective_id=0, has_side_effects=True, vmem_limit_bytes=60 * 1024 * 1024
        ),
        name="gram_and_products",
    )(descriptors, points)


def finish_kernel(
    total_rows, d_ref, p_ref, pp_ref, s_ref, linv_ref, q_ref, r_ref, t_ref, r_high, r_low
):
    joint = 2 * PANEL

    @pl.when(pl.program_id(0) == 0)
    def _():
        for block in range(r_ref.shape[1] // PANEL):
            cols = slice(block * PANEL, (block + 1) * PANEL)
            sums = s_ref[block * joint : (block + 1) * joint, :]
            value = dot_nn(linv_ref[...], sums, HIGHEST) / total_rows
            r_ref[:, cols] = value
            r_high[:, cols], r_low[:, cols] = split(value)

    dots = dot_nt(d_ref[...], pp_ref[...])
    q = dot_nt(dots * dots, linv_ref[...], HIGHEST)
    q_ref[...] = q
    q_high, q_low = split(q)
    for block in range(r_ref.shape[1] // joint):
        cols = slice(block * joint, (block + 1) * joint)
        dots = dot_nt(d_ref[...], p_ref[cols, :])
        change = three_pass(q_high, q_low, r_high[:, cols], r_low[:, cols])
        t_ref[:, cols] = (dots * dots - change).astype(BF16)


def finished(descriptors, points, panel_points, sums, inverse, total_rows):
    rows, width = descriptors.shape
    cols = points.shape[0]
    joint = 2 * PANEL
    tile = 256
    whole = lambda shape: pl.BlockSpec(shape, lambda i: (0, 0))
    tiled = lambda lanes: pl.BlockSpec((tile, lanes), lambda i: (i, 0))
    return pl.pallas_call(
        functools.partial(finish_kernel, total_rows),
        out_shape=(
            jax.ShapeDtypeStruct((rows, joint), F32),
            jax.ShapeDtypeStruct((joint, cols), F32),
            jax.ShapeDtypeStruct((rows, cols), BF16),
        ),
        grid=(rows // tile,),
        in_specs=[
            tiled(width),
            whole((cols, width)),
            whole((joint, width)),
            whole(sums.shape),
            whole((joint, joint)),
        ],
        out_specs=(tiled(joint), whole((joint, cols)), tiled(cols)),
        scratch_shapes=[pltpu.VMEM((joint, cols), BF16), pltpu.VMEM((joint, cols), BF16)],
        compiler_params=pltpu.CompilerParams(vmem_limit_bytes=40 * 1024 * 1024),
        name="factors_and_remainder",
    )(descriptors, points, panel_points, sums, inverse)


def solution(mesh):
    n_rows, n_cols = mesh.shape["rows"], mesh.shape["cols"]

    def on_device(descriptors, sparse_points):
        panel_points, sums, inverse = reduced(descriptors, sparse_points, n_rows, n_cols)
        total_rows = float(descriptors.shape[0] * n_rows)
        return finished(descriptors, sparse_points, panel_points, sums, inverse, total_rows)

    in_specs = (P("rows", None), P("cols", None))
    out_specs = (P("rows", None), P(None, "cols"), P("rows", "cols"))
    return jax.shard_map(
        on_device, mesh=mesh, in_specs=in_specs, out_specs=out_specs, check_vma=False
    )
```

```python
import functools

import jax
import jax.numpy as jnp
from jax import lax
from jax.experimental import pallas as pl
from jax.experimental.pallas import tpu as pltpu
from jax.sharding import PartitionSpec as P

PANEL = 128
BLOCK = 32
SUB = 8
LANES = 128
HIGHEST = lax.Precision.HIGHEST
F32 = jnp.float32
BF16 = jnp.bfloat16
MESH = pl.DeviceIdType.MESH


def dot_nt(a, b, precision=None):
    return lax.dot_general(
        a, b, (((1,), (1,)), ((), ())), precision=precision, preferred_element_type=F32
    )


def dot_nn(a, b, precision=None):
    return lax.dot_general(
        a, b, (((1,), (0,)), ((), ())), precision=precision, preferred_element_type=F32
    )


def dot_tn(a, b, precision=None):
    return lax.dot_general(
        a, b, (((0,), (0,)), ((), ())), precision=precision, preferred_element_type=F32
    )


def split(value):
    high = value.astype(BF16)
    return high, (value - high.astype(F32)).astype(BF16)


def three_pass(a_high, a_low, b_high, b_low):
    return dot_nn(a_high, b_high) + (dot_nn(a_high, b_low) + dot_nn(a_low, b_high))


def factor_block(tile, off):
    row = lax.broadcasted_iota(jnp.int32, (BLOCK, LANES), 0)
    lane = lax.broadcasted_iota(jnp.int32, (BLOCK, LANES), 1)
    inverse = jnp.where(row == lane, 1.0, 0.0).astype(F32)
    done = []
    for top in range(0, BLOCK, SUB):
        left = BLOCK - top
        rows = row[:left, :]
        columns = [
            jnp.broadcast_to(tile[:, off + top + j : off + top + j + 1], (left, LANES))
            for j in range(SUB)
        ]
        scale = jnp.ones((SUB, LANES), F32)
        for j in range(SUB):
            pivot = columns[j][j : j + 1, :]
            factor = jnp.where(rows > j, columns[j] * (1.0 / pivot), 0.0)
            for k in range(j + 1, SUB):
                columns[k] = columns[k] - factor * columns[k][j : j + 1, :]
            tile = tile - factor * tile[j : j + 1, :]
            inverse = inverse - factor * inverse[j : j + 1, :]
            scale = jnp.where(rows[:SUB] == j, lax.rsqrt(pivot), scale)
        done.append(inverse[:SUB] * scale)
        tile, inverse = tile[SUB:], inverse[SUB:]
    return jnp.concatenate(done, axis=0)[:, :BLOCK]


def factor_step(work, at):
    size = work.shape[0]
    tile_at = at // LANES * LANES
    rest = at + BLOCK
    start = min(rest // LANES * LANES, size)
    stop = size + -(-rest // LANES) * LANES
    factor = factor_block(work[at:rest, tile_at : tile_at + LANES], at - tile_at)
    panel = dot_nn(factor, work[at:rest, start:stop], HIGHEST)
    work[at:rest, start:stop] = panel
    if rest < size:
        turned = panel[:, : size - start].T
        for low, high in ((rest, rest + BLOCK), (rest + BLOCK, size)):
            if low < high:
                change = dot_nn(turned[low - start : high - start, :], panel, HIGHEST)
                work[low:high, start:stop] = work[low:high, start:stop] - change


def reduce_kernel(
    n_rows, n_cols, inner, total_rows,
    d_hbm, p_hbm, pp_ref, s_ref, linv_ref,
    d_ref, p_ref, pp, k_high, k_low, part, full, recv_one, recv_two, gram_one, gram_two, gram_own, gram, work,
    pp_send, pp_recv, sends, recvs, grams_send, grams_recv, swap_send, swap_recv, out_sem, in_sem,
):
    outer = n_rows // inner
    me_row, me_col = lax.axis_index("rows"), lax.axis_index("cols")
    me_in, me_out = lax.rem(me_row, inner), lax.div(me_row, inner)
    joint = 2 * PANEL
    blocks = part.shape[0] // joint

    def inner_peer(t):
        at = lax.rem(me_in + t, inner)
        return at, (me_out * inner + at, me_col)

    def outer_peer(t):
        at = lax.rem(me_out + t, outer)
        return at, (at * inner + me_in, me_col)

    barrier = pltpu.get_barrier_semaphore()
    for t in range(1, inner):
        pl.semaphore_signal(barrier, inc=1, device_id=inner_peer(t)[1], device_id_type=MESH)
    for t in range(1, outer):
        pl.semaphore_signal(barrier, inc=1, device_id=outer_peer(t)[1], device_id_type=MESH)
    for t in range(1, n_cols):
        to = lax.rem(me_col + t, n_cols)
        pl.semaphore_signal(barrier, inc=1, device_id=(me_row, to), device_id_type=MESH)
    load_d = pltpu.make_async_copy(d_hbm, d_ref, in_sem.at[0])
    load_p = pltpu.make_async_copy(p_hbm, p_ref, in_sem.at[1])
    load_p.start()
    load_d.start()
    pl.semaphore_wait(barrier, inner + outer + n_cols - 3)

    def share(source, target_of, send_sem, recv_sem, own):
        def copy(which, t):
            to = lax.rem(which + t, n_cols)
            return pltpu.make_async_remote_copy(
                src_ref=source, dst_ref=target_of(which),
                send_sem=send_sem.at[which, t - 1], recv_sem=recv_sem.at[which],
                device_id=(me_row, to), device_id_type=MESH,
            )

        def start():
            for which in range(2):
                @pl.when(me_col == which)
                def _():
                    for t in range(1, n_cols):
                        copy(which, t).start()

        def finish():
            for which in range(2):
                @pl.when(me_col == which)
                def _():
                    own(which)

                @pl.when(me_col != which)
                def _():
                    copy(which, 1).wait_recv()

        def drain():
            for which in range(2):
                @pl.when(me_col == which)
                def _():
                    for t in range(1, n_cols):
                        copy(which, t).wait_send()

        return start, finish, drain

    def own_points(which):
        pp[which * PANEL : (which + 1) * PANEL, :] = p_ref[:PANEL, :]

    points_start, points_finish, points_drain = share(
        p_hbm.at[pl.ds(0, PANEL)],
        lambda which: pp.at[pl.ds(which * PANEL, PANEL)],
        pp_send, pp_recv, own_points,
    )
    points_start()
    load_p.wait()
    load_d.wait()
    for block in range(blocks // 2):
        cols = slice(block * joint, (block + 1) * joint)
        dots = dot_nt(d_ref[...], p_ref[cols, :])
        k_high[:, cols], k_low[:, cols] = split(dots * dots)
    points_finish()
    dots = dot_nt(pp[...], d_ref[...])
    j_high, j_low = split(dots * dots)
    pp_ref[...] = pp[...]

    def products(block):
        cols = slice(block * joint, (block + 1) * joint)
        value = three_pass(j_high, j_low, k_high[:, cols], k_low[:, cols])
        part[block * 2 * joint : block * 2 * joint + joint, :] = value[:, :PANEL]
        part[block * 2 * joint + joint : (block + 1) * 2 * joint, :] = value[:, PANEL:]

    piece = joint // inner

    def gram_scatter(t):
        to, device = inner_peer(t)
        return pltpu.make_async_remote_copy(
            src_ref=part.at[pl.ds(pl.multiple_of(to * piece, 8), piece)],
            dst_ref=gram_one.at[t - 1],
            send_sem=grams_send.at[0, t - 1], recv_sem=grams_recv.at[0, t - 1],
            device_id=device, device_id_type=MESH,
        )

    def gram_exchange(t):
        device = outer_peer(t)[1]
        return pltpu.make_async_remote_copy(
            src_ref=gram_two.at[me_out], dst_ref=gram_two.at[me_out],
            send_sem=grams_send.at[1, t - 1], recv_sem=grams_recv.at[1, t - 1],
            device_id=device, device_id_type=MESH,
        )

    own_piece = pl.ds(pl.multiple_of(me_in * piece, 8), piece)

    def gram_gather(t):
        device = inner_peer(t)[1]
        return pltpu.make_async_remote_copy(
            src_ref=gram_own.at[own_piece], dst_ref=gram_own.at[own_piece],
            send_sem=grams_send.at[2, t - 1], recv_sem=grams_recv.at[2, t - 1],
            device_id=device, device_id_type=MESH,
        )

    products(0)
    for t in range(1, inner):
        gram_scatter(t).start()
    for block in range(1, blocks // 2):
        products(block)

    first = joint if (part.shape[0] - joint) % (16 * n_rows) == 0 else 0
    chunk = (part.shape[0] - first) // 2
    wide, narrow = chunk // inner, chunk // n_rows

    def bulk(c):
        base = first + c * chunk

        def wide_at(i):
            return pl.ds(pl.multiple_of(base + i * wide, 8), wide)

        def narrow_at(o):
            return pl.ds(pl.multiple_of(base + me_in * wide + o * narrow, 8), narrow)

        def copy(stage, t):
            to, device = (inner_peer if stage in (0, 3) else outer_peer)(t)
            source, target = (
                (lambda: (part.at[wide_at(to)], recv_one.at[c, t - 1])),
                (lambda: (part.at[narrow_at(to)], recv_two.at[c, t - 1])),
                (lambda: (full.at[narrow_at(me_out)],) * 2),
                (lambda: (full.at[wide_at(me_in)],) * 2),
            )[stage]()
            return pltpu.make_async_remote_copy(
                src_ref=source, dst_ref=target,
                send_sem=sends.at[c, stage, t - 1], recv_sem=recvs.at[c, stage, t - 1],
                device_id=device, device_id_type=MESH,
            )

        def copies(stage):
            return [copy(stage, t) for t in range(1, inner if stage in (0, 3) else outer)]

        def start(stage):
            for one in copies(stage):
                one.start()

        def step(stage):
            for one in copies(stage):
                one.wait_recv()
            if stage == 0:
                for one in copies(stage):
                    one.wait_send()
                value = part[wide_at(me_in), :]
                for t in range(inner - 1):
                    value = value + recv_one[c, t]
                part[wide_at(me_in), :] = value
            if stage == 1:
                value = part[narrow_at(me_out), :]
                for t in range(outer - 1):
                    value = value + recv_two[c, t]
                full[narrow_at(me_out), :] = value
            if stage < 3:
                start(stage + 1)

        def drain():
            for stage in range(1, 4):
                for one in copies(stage):
                    one.wait_send()

        return start, step, drain

    (start_a, step_a, drain_a), (start_b, step_b, drain_b) = bulk(0), bulk(1)
    start_a(0)
    start_b(0)

    for t in range(1, inner):
        gram_scatter(t).wait_recv()
    value = part[own_piece, :]
    for t in range(inner - 1):
        value = value + gram_one[t]
    gram_two[me_out] = value
    for t in range(1, outer):
        gram_exchange(t).start()
    for t in range(1, inner):
        gram_scatter(t).wait_send()
    for t in range(1, outer):
        gram_exchange(t).wait_recv()
    value = gram_two[0]
    for o in range(1, outer):
        value = value + gram_two[o]
    gram_own[own_piece, :] = value
    for t in range(1, inner):
        gram_gather(t).start()
    step_a(0)
    for t in range(1, inner):
        gram_gather(t).wait_recv()

    def own_gram(which):
        gram[which] = gram_own[...]

    gram_start, gram_finish, gram_drain = share(
        gram_own, lambda which: gram.at[which], swap_send, swap_recv, own_gram
    )
    gram_start()
    step_b(0)
    gram_finish()
    work[:, :PANEL] = gram[0] / total_rows
    work[:, PANEL:joint] = gram[1] / total_rows
    row = lax.broadcasted_iota(jnp.int32, (joint, joint), 0)
    lane = lax.broadcasted_iota(jnp.int32, (joint, joint), 1)
    work[:, joint:] = jnp.where(row == lane, 1.0, 0.0).astype(F32)

    pending = [
        functools.partial(step, stage) for stage in range(1, 4) for step in (step_a, step_b)
    ]
    for at in range(0, joint, BLOCK):
        factor_step(work, at)
        if pending:
            pending.pop(0)()
    linv_ref[...] = work[:, joint:]
    for step in pending:
        step()
    rest = pl.ds(first, part.shape[0] - first)
    results = [pltpu.make_async_copy(full.at[rest], s_ref.at[rest], out_sem.at[0])]
    if first > 0:
        head = s_ref.at[pl.ds(0, joint)]
        results.append(pltpu.make_async_copy(gram_own, head, out_sem.at[1]))
    for result in results:
        result.start()
    points_drain()
    gram_drain()
    for t in range(1, outer):
        gram_exchange(t).wait_send()
    for t in range(1, inner):
        gram_gather(t).wait_send()
    drain_a()
    drain_b()
    for result in results:
        result.wait()


def reduced(descriptors, points, n_rows, n_cols):
    rows, width = descriptors.shape
    cols = points.shape[0]
    joint = 2 * PANEL
    inner = 4 if n_rows % 4 == 0 else 1
    outer = n_rows // inner
    flat = cols // PANEL * joint
    first = joint if (flat - joint) % (16 * n_rows) == 0 else 0
    chunk = (flat - first) // 2
    most = max(inner, outer, 2) - 1
    vmem = pl.BlockSpec(memory_space=pltpu.VMEM)
    dma = pltpu.SemaphoreType.DMA
    return pl.pallas_call(
        functools.partial(reduce_kernel, n_rows, n_cols, inner, float(rows * n_rows)),
        out_shape=(
            jax.ShapeDtypeStruct((joint, width), BF16),
            jax.ShapeDtypeStruct((flat, PANEL), F32),
            jax.ShapeDtypeStruct((joint, joint), F32),
        ),
        in_specs=[pl.BlockSpec(memory_space=pltpu.HBM)] * 2,
        out_specs=(vmem, pl.BlockSpec(memory_space=pl.ANY), vmem),
        scratch_shapes=[
            pltpu.VMEM((rows, width), BF16),
            pltpu.VMEM((cols, width), BF16),
            pltpu.VMEM((joint, width), BF16),
            pltpu.VMEM((rows, cols), BF16),
            pltpu.VMEM((rows, cols), BF16),
            pltpu.VMEM((flat, PANEL), F32),
            pltpu.VMEM((flat, PANEL), F32),
            pltpu.VMEM((2, inner - 1, chunk // inner, PANEL), F32),
            pltpu.VMEM((2, outer - 1, chunk // n_rows, PANEL), F32),
            pltpu.VMEM((inner - 1, joint // inner, PANEL), F32),
            pltpu.VMEM((outer, joint // inner, PANEL), F32),
            pltpu.VMEM((joint, PANEL), F32),
            pltpu.VMEM((2, joint, PANEL), F32),
            pltpu.VMEM((joint, 2 * joint), F32),
            dma((2, n_cols - 1)),
            dma((2,)),
            dma((2, 4, most)),
            dma((2, 4, most)),
            dma((3, most)),
            dma((3, most)),
            dma((2, n_cols - 1)),
            dma((2,)),
            dma((2,)),
            dma((2,)),
        ],
        compiler_params=pltpu.CompilerParams(
            collective_id=0, has_side_effects=True, vmem_limit_bytes=60 * 1024 * 1024
        ),
        name="gram_and_products",
    )(descriptors, points)


def finish_kernel(
    total_rows, d_ref, p_ref, pp_ref, s_ref, linv_ref, q_ref, r_ref, t_ref, r_high, r_low
):
    joint = 2 * PANEL

    @pl.when(pl.program_id(0) == 0)
    def _():
        for block in range(r_ref.shape[1] // PANEL):
            cols = slice(block * PANEL, (block + 1) * PANEL)
            sums = s_ref[block * joint : (block + 1) * joint, :]
            value = dot_nn(linv_ref[...], sums, HIGHEST) / total_rows
            r_ref[:, cols] = value
            r_high[:, cols], r_low[:, cols] = split(value)

    dots = dot_nt(d_ref[...], pp_ref[...])
    q = dot_nt(dots * dots, linv_ref[...], HIGHEST)
    q_ref[...] = q
    q_high, q_low = split(q)
    for block in range(r_ref.shape[1] // joint):
        cols = slice(block * joint, (block + 1) * joint)
        dots = dot_nt(d_ref[...], p_ref[cols, :])
        change = three_pass(q_high, q_low, r_high[:, cols], r_low[:, cols])
        t_ref[:, cols] = (dots * dots - change).astype(BF16)


def finished(descriptors, points, panel_points, sums, inverse, total_rows):
    rows, width = descriptors.shape
    cols = points.shape[0]
    joint = 2 * PANEL
    tile = 256
    whole = lambda shape: pl.BlockSpec(shape, lambda i: (0, 0))
    tiled = lambda lanes: pl.BlockSpec((tile, lanes), lambda i: (i, 0))
    return pl.pallas_call(
        functools.partial(finish_kernel, total_rows),
        out_shape=(
            jax.ShapeDtypeStruct((rows, joint), F32),
            jax.ShapeDtypeStruct((joint, cols), F32),
            jax.ShapeDtypeStruct((rows, cols), BF16),
        ),
        grid=(rows // tile,),
        in_specs=[
            tiled(width),
            whole((cols, width)),
            whole((joint, width)),
            whole(sums.shape),
            whole((joint, joint)),
        ],
        out_specs=(tiled(joint), whole((joint, cols)), tiled(cols)),
        scratch_shapes=[pltpu.VMEM((joint, cols), BF16), pltpu.VMEM((joint, cols), BF16)],
        compiler_params=pltpu.CompilerParams(vmem_limit_bytes=60 * 1024 * 1024),
        name="factors_and_remainder",
    )(descriptors, points, panel_points, sums, inverse)


def solution(mesh):
    n_rows, n_cols = mesh.shape["rows"], mesh.shape["cols"]

    def on_device(descriptors, sparse_points):
        panel_points, sums, inverse = reduced(descriptors, sparse_points, n_rows, n_cols)
        total_rows = float(descriptors.shape[0] * n_rows)
        return finished(descriptors, sparse_points, panel_points, sums, inverse, total_rows)

    in_specs = (P("rows", None), P("cols", None))
    out_specs = (P("rows", None), P(None, "cols"), P("rows", "cols"))
    return jax.shard_map(
        on_device, mesh=mesh, in_specs=in_specs, out_specs=out_specs, check_vma=False
    )
```

```python
import functools

import jax
import jax.numpy as jnp
from jax import lax
from jax.experimental import pallas as pl
from jax.experimental.pallas import tpu as pltpu
from jax.sharding import PartitionSpec as P

PANEL = 128
BLOCK = 32
SUB = 8
LANES = 128
HIGHEST = lax.Precision.HIGHEST
F32 = jnp.float32
BF16 = jnp.bfloat16
MESH = pl.DeviceIdType.MESH


def dot_nt(a, b, precision=None):
    return lax.dot_general(
        a, b, (((1,), (1,)), ((), ())), precision=precision, preferred_element_type=F32
    )


def dot_nn(a, b, precision=None):
    return lax.dot_general(
        a, b, (((1,), (0,)), ((), ())), precision=precision, preferred_element_type=F32
    )


def dot_tn(a, b, precision=None):
    return lax.dot_general(
        a, b, (((0,), (0,)), ((), ())), precision=precision, preferred_element_type=F32
    )


def split(value):
    high = value.astype(BF16)
    return high, (value - high.astype(F32)).astype(BF16)


def three_pass(a_high, a_low, b_high, b_low):
    return dot_nn(a_high, b_high) + (dot_nn(a_high, b_low) + dot_nn(a_low, b_high))


def factor_block(tile, off):
    row = lax.broadcasted_iota(jnp.int32, (BLOCK, LANES), 0)
    lane = lax.broadcasted_iota(jnp.int32, (BLOCK, LANES), 1)
    inverse = jnp.where(row == lane, 1.0, 0.0).astype(F32)
    done = []
    for top in range(0, BLOCK, SUB):
        left = BLOCK - top
        rows = row[:left, :]
        columns = [
            jnp.broadcast_to(tile[:, off + top + j : off + top + j + 1], (left, LANES))
            for j in range(SUB)
        ]
        scale = jnp.ones((SUB, LANES), F32)
        for j in range(SUB):
            root = lax.rsqrt(columns[j][j : j + 1, :])
            reciprocal = root * root
            for k in range(j + 1, SUB):
                columns[k] = columns[k] - (columns[j] * columns[k][j : j + 1, :]) * reciprocal
            factor = jnp.where(rows > j, columns[j] * reciprocal, 0.0)
            tile = tile - factor * tile[j : j + 1, :]
            inverse = inverse - factor * inverse[j : j + 1, :]
            scale = jnp.where(rows[:SUB] == j, root, scale)
        done.append(inverse[:SUB] * scale)
        tile, inverse = tile[SUB:], inverse[SUB:]
    return jnp.concatenate(done, axis=0)[:, :BLOCK]


def factor_step(work, at):
    size = work.shape[0]
    tile_at = at // LANES * LANES
    rest = at + BLOCK
    start = min(rest // LANES * LANES, size)
    stop = size + -(-rest // LANES) * LANES
    factor = factor_block(work[at:rest, tile_at : tile_at + LANES], at - tile_at)
    panel = dot_nn(factor, work[at:rest, start:stop], HIGHEST)
    work[at:rest, start:stop] = panel
    if rest < size:
        turned = panel[:, : size - start].T
        for low, high in ((rest, rest + BLOCK), (rest + BLOCK, size)):
            if low < high:
                change = dot_nn(turned[low - start : high - start, :], panel, HIGHEST)
                work[low:high, start:stop] = work[low:high, start:stop] - change


def reduce_kernel(
    n_rows, n_cols, inner, total_rows,
    d_hbm, p_hbm, pp_ref, s_ref, linv_ref,
    d_ref, p_ref, pp, k_high, k_low, part, full, recv_one, recv_two, gram_one, gram_two, gram_own, gram, work,
    pp_send, pp_recv, sends, recvs, grams_send, grams_recv, swap_send, swap_recv, out_sem, in_sem,
):
    outer = n_rows // inner
    me_row, me_col = lax.axis_index("rows"), lax.axis_index("cols")
    me_in, me_out = lax.rem(me_row, inner), lax.div(me_row, inner)
    joint = 2 * PANEL
    blocks = part.shape[0] // joint

    def inner_peer(t):
        at = lax.rem(me_in + t, inner)
        return at, (me_out * inner + at, me_col)

    def outer_peer(t):
        at = lax.rem(me_out + t, outer)
        return at, (at * inner + me_in, me_col)

    barrier = pltpu.get_barrier_semaphore()
    for t in range(1, inner):
        pl.semaphore_signal(barrier, inc=1, device_id=inner_peer(t)[1], device_id_type=MESH)
    for t in range(1, outer):
        pl.semaphore_signal(barrier, inc=1, device_id=outer_peer(t)[1], device_id_type=MESH)
    for t in range(1, n_cols):
        to = lax.rem(me_col + t, n_cols)
        pl.semaphore_signal(barrier, inc=1, device_id=(me_row, to), device_id_type=MESH)
    load_d = pltpu.make_async_copy(d_hbm, d_ref, in_sem.at[0])
    load_p = pltpu.make_async_copy(p_hbm, p_ref, in_sem.at[1])
    load_p.start()
    load_d.start()
    pl.semaphore_wait(barrier, inner + outer + n_cols - 3)

    def share(source, target_of, send_sem, recv_sem, own):
        def copy(which, t):
            to = lax.rem(which + t, n_cols)
            return pltpu.make_async_remote_copy(
                src_ref=source, dst_ref=target_of(which),
                send_sem=send_sem.at[which, t - 1], recv_sem=recv_sem.at[which],
                device_id=(me_row, to), device_id_type=MESH,
            )

        def start():
            for which in range(2):
                @pl.when(me_col == which)
                def _():
                    for t in range(1, n_cols):
                        copy(which, t).start()

        def finish():
            for which in range(2):
                @pl.when(me_col == which)
                def _():
                    own(which)

                @pl.when(me_col != which)
                def _():
                    copy(which, 1).wait_recv()

        def drain():
            for which in range(2):
                @pl.when(me_col == which)
                def _():
                    for t in range(1, n_cols):
                        copy(which, t).wait_send()

        return start, finish, drain

    def own_points(which):
        pp[which * PANEL : (which + 1) * PANEL, :] = p_ref[:PANEL, :]

    points_start, points_finish, points_drain = share(
        p_hbm.at[pl.ds(0, PANEL)],
        lambda which: pp.at[pl.ds(which * PANEL, PANEL)],
        pp_send, pp_recv, own_points,
    )
    points_start()
    load_p.wait()
    load_d.wait()
    for block in range(blocks // 2):
        cols = slice(block * joint, (block + 1) * joint)
        dots = dot_nt(d_ref[...], p_ref[cols, :])
        k_high[:, cols], k_low[:, cols] = split(dots * dots)
    points_finish()
    dots = dot_nt(pp[...], d_ref[...])
    j_high, j_low = split(dots * dots)
    pp_ref[...] = pp[...]

    def products(block):
        cols = slice(block * joint, (block + 1) * joint)
        value = three_pass(j_high, j_low, k_high[:, cols], k_low[:, cols])
        part[block * 2 * joint : block * 2 * joint + joint, :] = value[:, :PANEL]
        part[block * 2 * joint + joint : (block + 1) * 2 * joint, :] = value[:, PANEL:]

    piece = joint // inner

    def gram_scatter(t):
        to, device = inner_peer(t)
        return pltpu.make_async_remote_copy(
            src_ref=part.at[pl.ds(pl.multiple_of(to * piece, 8), piece)],
            dst_ref=gram_one.at[t - 1],
            send_sem=grams_send.at[0, t - 1], recv_sem=grams_recv.at[0, t - 1],
            device_id=device, device_id_type=MESH,
        )

    def gram_exchange(t):
        device = outer_peer(t)[1]
        return pltpu.make_async_remote_copy(
            src_ref=gram_two.at[me_out], dst_ref=gram_two.at[me_out],
            send_sem=grams_send.at[1, t - 1], recv_sem=grams_recv.at[1, t - 1],
            device_id=device, device_id_type=MESH,
        )

    own_piece = pl.ds(pl.multiple_of(me_in * piece, 8), piece)

    def gram_gather(t):
        device = inner_peer(t)[1]
        return pltpu.make_async_remote_copy(
            src_ref=gram_own.at[own_piece], dst_ref=gram_own.at[own_piece],
            send_sem=grams_send.at[2, t - 1], recv_sem=grams_recv.at[2, t - 1],
            device_id=device, device_id_type=MESH,
        )

    products(0)
    for t in range(1, inner):
        gram_scatter(t).start()
    for block in range(1, blocks // 2):
        products(block)

    first = joint if (part.shape[0] - joint) % (16 * n_rows) == 0 else 0
    chunk = (part.shape[0] - first) // 2
    wide, narrow = chunk // inner, chunk // n_rows

    def bulk(c):
        base = first + c * chunk

        def wide_at(i):
            return pl.ds(pl.multiple_of(base + i * wide, 8), wide)

        def narrow_at(o):
            return pl.ds(pl.multiple_of(base + me_in * wide + o * narrow, 8), narrow)

        def copy(stage, t):
            to, device = (inner_peer if stage in (0, 3) else outer_peer)(t)
            source, target = (
                (lambda: (part.at[wide_at(to)], recv_one.at[c, t - 1])),
                (lambda: (part.at[narrow_at(to)], recv_two.at[c, t - 1])),
                (lambda: (full.at[narrow_at(me_out)],) * 2),
                (lambda: (full.at[wide_at(me_in)],) * 2),
            )[stage]()
            return pltpu.make_async_remote_copy(
                src_ref=source, dst_ref=target,
                send_sem=sends.at[c, stage, t - 1], recv_sem=recvs.at[c, stage, t - 1],
                device_id=device, device_id_type=MESH,
            )

        def copies(stage):
            return [copy(stage, t) for t in range(1, inner if stage in (0, 3) else outer)]

        def start(stage):
            for one in copies(stage):
                one.start()

        def step(stage):
            for one in copies(stage):
                one.wait_recv()
            if stage == 0:
                for one in copies(stage):
                    one.wait_send()
                value = part[wide_at(me_in), :]
                for t in range(inner - 1):
                    value = value + recv_one[c, t]
                part[wide_at(me_in), :] = value
            if stage == 1:
                value = part[narrow_at(me_out), :]
                for t in range(outer - 1):
                    value = value + recv_two[c, t]
                full[narrow_at(me_out), :] = value
            if stage < 3:
                start(stage + 1)

        def drain():
            for stage in range(1, 4):
                for one in copies(stage):
                    one.wait_send()

        return start, step, drain

    (start_a, step_a, drain_a), (start_b, step_b, drain_b) = bulk(0), bulk(1)
    start_a(0)
    start_b(0)

    for t in range(1, inner):
        gram_scatter(t).wait_recv()
    value = part[own_piece, :]
    for t in range(inner - 1):
        value = value + gram_one[t]
    gram_two[me_out] = value
    for t in range(1, outer):
        gram_exchange(t).start()
    for t in range(1, inner):
        gram_scatter(t).wait_send()
    for t in range(1, outer):
        gram_exchange(t).wait_recv()
    value = gram_two[0]
    for o in range(1, outer):
        value = value + gram_two[o]
    gram_own[own_piece, :] = value
    for t in range(1, inner):
        gram_gather(t).start()
    step_a(0)
    for t in range(1, inner):
        gram_gather(t).wait_recv()

    def own_gram(which):
        gram[which] = gram_own[...]

    gram_start, gram_finish, gram_drain = share(
        gram_own, lambda which: gram.at[which], swap_send, swap_recv, own_gram
    )
    gram_start()
    results = []
    if first > 0:
        head = s_ref.at[pl.ds(0, joint)]
        results.append(pltpu.make_async_copy(gram_own, head, out_sem.at[2]))
        results[-1].start()
    step_b(0)
    gram_finish()
    work[:, :PANEL] = gram[0] / total_rows
    work[:, PANEL:joint] = gram[1] / total_rows
    row = lax.broadcasted_iota(jnp.int32, (joint, joint), 0)
    lane = lax.broadcasted_iota(jnp.int32, (joint, joint), 1)
    work[:, joint:] = jnp.where(row == lane, 1.0, 0.0).astype(F32)

    pending = [
        functools.partial(step, stage) for stage in range(1, 4) for step in (step_a, step_b)
    ]
    for at in range(0, joint, BLOCK):
        factor_step(work, at)
        if len(pending) > 2:
            pending.pop(0)()
    linv_ref[...] = work[:, joint:]
    for step in pending[:-2]:
        step()
    for c, step in enumerate((step_a, step_b)):
        step(3)
        rows = pl.ds(first + c * chunk, chunk)
        results.append(pltpu.make_async_copy(full.at[rows], s_ref.at[rows], out_sem.at[c]))
        results[-1].start()
    points_drain()
    gram_drain()
    for t in range(1, outer):
        gram_exchange(t).wait_send()
    for t in range(1, inner):
        gram_gather(t).wait_send()
    drain_a()
    drain_b()
    for result in results:
        result.wait()


def reduced(descriptors, points, n_rows, n_cols):
    rows, width = descriptors.shape
    cols = points.shape[0]
    joint = 2 * PANEL
    inner = 4 if n_rows % 4 == 0 else 1
    outer = n_rows // inner
    flat = cols // PANEL * joint
    first = joint if (flat - joint) % (16 * n_rows) == 0 else 0
    chunk = (flat - first) // 2
    most = max(inner, outer, 2) - 1
    vmem = pl.BlockSpec(memory_space=pltpu.VMEM)
    dma = pltpu.SemaphoreType.DMA
    return pl.pallas_call(
        functools.partial(reduce_kernel, n_rows, n_cols, inner, float(rows * n_rows)),
        out_shape=(
            jax.ShapeDtypeStruct((joint, width), BF16),
            jax.ShapeDtypeStruct((flat, PANEL), F32),
            jax.ShapeDtypeStruct((joint, joint), F32),
        ),
        in_specs=[pl.BlockSpec(memory_space=pltpu.HBM)] * 2,
        out_specs=(vmem, pl.BlockSpec(memory_space=pl.ANY), vmem),
        scratch_shapes=[
            pltpu.VMEM((rows, width), BF16),
            pltpu.VMEM((cols, width), BF16),
            pltpu.VMEM((joint, width), BF16),
            pltpu.VMEM((rows, cols), BF16),
            pltpu.VMEM((rows, cols), BF16),
            pltpu.VMEM((flat, PANEL), F32),
            pltpu.VMEM((flat, PANEL), F32),
            pltpu.VMEM((2, inner - 1, chunk // inner, PANEL), F32),
            pltpu.VMEM((2, outer - 1, chunk // n_rows, PANEL), F32),
            pltpu.VMEM((inner - 1, joint // inner, PANEL), F32),
            pltpu.VMEM((outer, joint // inner, PANEL), F32),
            pltpu.VMEM((joint, PANEL), F32),
            pltpu.VMEM((2, joint, PANEL), F32),
            pltpu.VMEM((joint, 2 * joint), F32),
            dma((2, n_cols - 1)),
            dma((2,)),
            dma((2, 4, most)),
            dma((2, 4, most)),
            dma((3, most)),
            dma((3, most)),
            dma((2, n_cols - 1)),
            dma((2,)),
            dma((3,)),
            dma((2,)),
        ],
        compiler_params=pltpu.CompilerParams(
            collective_id=0, has_side_effects=True, vmem_limit_bytes=60 * 1024 * 1024
        ),
        name="gram_and_products",
    )(descriptors, points)


def finish_kernel(
    total_rows, d_ref, p_ref, pp_ref, s_ref, linv_ref, q_ref, r_ref, t_ref, r_high, r_low
):
    joint = 2 * PANEL

    @pl.when(pl.program_id(0) == 0)
    def _():
        for block in range(r_ref.shape[1] // joint):
            cols = slice(block * joint, (block + 1) * joint)
            at = block * 2 * joint
            halves = (s_ref[at : at + joint, :], s_ref[at + joint : at + 2 * joint, :])
            sums = jnp.concatenate(halves, axis=1)
            value = dot_nn(linv_ref[...], sums, HIGHEST) / total_rows
            r_ref[:, cols] = value
            r_high[:, cols], r_low[:, cols] = split(value)

    dots = dot_nt(d_ref[...], pp_ref[...])
    q = dot_nt(dots * dots, linv_ref[...], HIGHEST)
    q_ref[...] = q
    q_high, q_low = split(q)
    for block in range(r_ref.shape[1] // joint):
        cols = slice(block * joint, (block + 1) * joint)
        dots = dot_nt(d_ref[...], p_ref[cols, :])
        change = three_pass(q_high, q_low, r_high[:, cols], r_low[:, cols])
        t_ref[:, cols] = (dots * dots - change).astype(BF16)


def finished(descriptors, points, panel_points, sums, inverse, total_rows):
    rows, width = descriptors.shape
    cols = points.shape[0]
    joint = 2 * PANEL
    tile = 256
    whole = lambda shape: pl.BlockSpec(shape, lambda i: (0, 0))
    tiled = lambda lanes: pl.BlockSpec((tile, lanes), lambda i: (i, 0))
    return pl.pallas_call(
        functools.partial(finish_kernel, total_rows),
        out_shape=(
            jax.ShapeDtypeStruct((rows, joint), F32),
            jax.ShapeDtypeStruct((joint, cols), F32),
            jax.ShapeDtypeStruct((rows, cols), BF16),
        ),
        grid=(rows // tile,),
        in_specs=[
            tiled(width),
            whole((cols, width)),
            whole((joint, width)),
            whole(sums.shape),
            whole((joint, joint)),
        ],
        out_specs=(tiled(joint), whole((joint, cols)), tiled(cols)),
        scratch_shapes=[pltpu.VMEM((joint, cols), BF16), pltpu.VMEM((joint, cols), BF16)],
        compiler_params=pltpu.CompilerParams(vmem_limit_bytes=60 * 1024 * 1024),
        name="factors_and_remainder",
    )(descriptors, points, panel_points, sums, inverse)


def solution(mesh):
    n_rows, n_cols = mesh.shape["rows"], mesh.shape["cols"]

    def on_device(descriptors, sparse_points):
        panel_points, sums, inverse = reduced(descriptors, sparse_points, n_rows, n_cols)
        total_rows = float(descriptors.shape[0] * n_rows)
        return finished(descriptors, sparse_points, panel_points, sums, inverse, total_rows)

    in_specs = (P("rows", None), P("cols", None))
    out_specs = (P("rows", None), P(None, "cols"), P("rows", "cols"))
    return jax.shard_map(
        on_device, mesh=mesh, in_specs=in_specs, out_specs=out_specs, check_vma=False
    )
```

```python
import functools

import jax
import jax.numpy as jnp
from jax import lax
from jax.experimental import pallas as pl
from jax.experimental.pallas import tpu as pltpu
from jax.sharding import PartitionSpec as P

PANEL = 128
BLOCK = 64
SUB = 8
LANES = 128
HIGHEST = lax.Precision.HIGHEST
F32 = jnp.float32
BF16 = jnp.bfloat16
MESH = pl.DeviceIdType.MESH


def dot_nt(a, b, precision=None):
    return lax.dot_general(
        a, b, (((1,), (1,)), ((), ())), precision=precision, preferred_element_type=F32
    )


def dot_nn(a, b, precision=None):
    return lax.dot_general(
        a, b, (((1,), (0,)), ((), ())), precision=precision, preferred_element_type=F32
    )


def dot_tn(a, b, precision=None):
    return lax.dot_general(
        a, b, (((0,), (0,)), ((), ())), precision=precision, preferred_element_type=F32
    )


def split(value):
    high = value.astype(BF16)
    return high, (value - high.astype(F32)).astype(BF16)


def three_pass(a_high, a_low, b_high, b_low):
    return dot_nn(a_high, b_high) + (dot_nn(a_high, b_low) + dot_nn(a_low, b_high))


def factor_block(tile, off):
    row = lax.broadcasted_iota(jnp.int32, (BLOCK, LANES), 0)
    lane = lax.broadcasted_iota(jnp.int32, (BLOCK, LANES), 1)
    inverse = jnp.where(row == lane, 1.0, 0.0).astype(F32)
    done = []
    for top in range(0, BLOCK, SUB):
        left = BLOCK - top
        rows = row[:left, :]
        columns = [
            jnp.broadcast_to(tile[:, off + top + j : off + top + j + 1], (left, LANES))
            for j in range(SUB)
        ]
        scale = jnp.ones((SUB, LANES), F32)
        for j in range(SUB):
            root = lax.rsqrt(columns[j][j : j + 1, :])
            reciprocal = root * root
            for k in range(j + 1, SUB):
                columns[k] = columns[k] - (columns[j] * columns[k][j : j + 1, :]) * reciprocal
            factor = jnp.where(rows > j, columns[j] * reciprocal, 0.0)
            tile = tile - factor * tile[j : j + 1, :]
            inverse = inverse - factor * inverse[j : j + 1, :]
            scale = jnp.where(rows[:SUB] == j, root, scale)
        done.append(inverse[:SUB] * scale)
        tile, inverse = tile[SUB:], inverse[SUB:]
    return jnp.concatenate(done, axis=0)[:, :BLOCK]


def factor_step(work, at):
    size = work.shape[0]
    tile_at = at // LANES * LANES
    rest = at + BLOCK
    start = min(rest // LANES * LANES, size)
    stop = size + -(-rest // LANES) * LANES
    factor = factor_block(work[at:rest, tile_at : tile_at + LANES], at - tile_at)
    panel = dot_nn(factor, work[at:rest, start:stop], HIGHEST)
    work[at:rest, start:stop] = panel
    if rest < size:
        turned = panel[:, : size - start].T
        for low, high in ((rest, rest + BLOCK), (rest + BLOCK, size)):
            if low < high:
                change = dot_nn(turned[low - start : high - start, :], panel, HIGHEST)
                work[low:high, start:stop] = work[low:high, start:stop] - change


def reduce_kernel(
    n_rows, n_cols, inner, total_rows,
    d_hbm, p_hbm, pp_ref, s_ref, linv_ref,
    d_ref, p_ref, pp, k_high, k_low, part, full, recv_one, recv_two, gram_one, gram_two, gram_own, gram, work,
    pp_send, pp_recv, sends, recvs, grams_send, grams_recv, swap_send, swap_recv, out_sem, in_sem,
):
    outer = n_rows // inner
    me_row, me_col = lax.axis_index("rows"), lax.axis_index("cols")
    me_in, me_out = lax.rem(me_row, inner), lax.div(me_row, inner)
    joint = 2 * PANEL
    blocks = part.shape[0] // joint

    def inner_peer(t):
        at = lax.rem(me_in + t, inner)
        return at, (me_out * inner + at, me_col)

    def outer_peer(t):
        at = lax.rem(me_out + t, outer)
        return at, (at * inner + me_in, me_col)

    barrier = pltpu.get_barrier_semaphore()
    for t in range(1, inner):
        pl.semaphore_signal(barrier, inc=1, device_id=inner_peer(t)[1], device_id_type=MESH)
    for t in range(1, outer):
        pl.semaphore_signal(barrier, inc=1, device_id=outer_peer(t)[1], device_id_type=MESH)
    for t in range(1, n_cols):
        to = lax.rem(me_col + t, n_cols)
        pl.semaphore_signal(barrier, inc=1, device_id=(me_row, to), device_id_type=MESH)
    load_d = pltpu.make_async_copy(d_hbm, d_ref, in_sem.at[0])
    load_p = pltpu.make_async_copy(p_hbm, p_ref, in_sem.at[1])
    load_p.start()
    load_d.start()
    pl.semaphore_wait(barrier, inner + outer + n_cols - 3)

    def share(source, target_of, send_sem, recv_sem, own):
        def copy(which, t):
            to = lax.rem(which + t, n_cols)
            return pltpu.make_async_remote_copy(
                src_ref=source, dst_ref=target_of(which),
                send_sem=send_sem.at[which, t - 1], recv_sem=recv_sem.at[which],
                device_id=(me_row, to), device_id_type=MESH,
            )

        def start():
            for which in range(2):
                @pl.when(me_col == which)
                def _():
                    for t in range(1, n_cols):
                        copy(which, t).start()

        def finish():
            for which in range(2):
                @pl.when(me_col == which)
                def _():
                    own(which)

                @pl.when(me_col != which)
                def _():
                    copy(which, 1).wait_recv()

        def drain():
            for which in range(2):
                @pl.when(me_col == which)
                def _():
                    for t in range(1, n_cols):
                        copy(which, t).wait_send()

        return start, finish, drain

    def own_points(which):
        pp[which * PANEL : (which + 1) * PANEL, :] = p_ref[:PANEL, :]

    points_start, points_finish, points_drain = share(
        p_hbm.at[pl.ds(0, PANEL)],
        lambda which: pp.at[pl.ds(which * PANEL, PANEL)],
        pp_send, pp_recv, own_points,
    )
    points_start()
    load_p.wait()
    load_d.wait()
    for block in range(blocks // 2):
        cols = slice(block * joint, (block + 1) * joint)
        dots = dot_nt(d_ref[...], p_ref[cols, :])
        k_high[:, cols], k_low[:, cols] = split(dots * dots)
    points_finish()
    dots = dot_nt(pp[...], d_ref[...])
    j_high, j_low = split(dots * dots)
    pp_ref[...] = pp[...]

    def products(block):
        cols = slice(block * joint, (block + 1) * joint)
        value = three_pass(j_high, j_low, k_high[:, cols], k_low[:, cols])
        part[block * 2 * joint : block * 2 * joint + joint, :] = value[:, :PANEL]
        part[block * 2 * joint + joint : (block + 1) * 2 * joint, :] = value[:, PANEL:]

    piece = joint // inner

    def gram_scatter(t):
        to, device = inner_peer(t)
        return pltpu.make_async_remote_copy(
            src_ref=part.at[pl.ds(pl.multiple_of(to * piece, 8), piece)],
            dst_ref=gram_one.at[t - 1],
            send_sem=grams_send.at[0, t - 1], recv_sem=grams_recv.at[0, t - 1],
            device_id=device, device_id_type=MESH,
        )

    def gram_exchange(t):
        device = outer_peer(t)[1]
        return pltpu.make_async_remote_copy(
            src_ref=gram_two.at[me_out], dst_ref=gram_two.at[me_out],
            send_sem=grams_send.at[1, t - 1], recv_sem=grams_recv.at[1, t - 1],
            device_id=device, device_id_type=MESH,
        )

    own_piece = pl.ds(pl.multiple_of(me_in * piece, 8), piece)

    def gram_gather(t):
        device = inner_peer(t)[1]
        return pltpu.make_async_remote_copy(
            src_ref=gram_own.at[own_piece], dst_ref=gram_own.at[own_piece],
            send_sem=grams_send.at[2, t - 1], recv_sem=grams_recv.at[2, t - 1],
            device_id=device, device_id_type=MESH,
        )

    products(0)
    for t in range(1, inner):
        gram_scatter(t).start()
    for block in range(1, blocks // 2):
        products(block)

    first = joint if (part.shape[0] - joint) % (16 * n_rows) == 0 else 0
    chunk = (part.shape[0] - first) // 2
    wide, narrow = chunk // inner, chunk // n_rows

    def bulk(c):
        base = first + c * chunk

        def wide_at(i):
            return pl.ds(pl.multiple_of(base + i * wide, 8), wide)

        def narrow_at(o):
            return pl.ds(pl.multiple_of(base + me_in * wide + o * narrow, 8), narrow)

        def copy(stage, t):
            to, device = (inner_peer if stage in (0, 3) else outer_peer)(t)
            source, target = (
                (lambda: (part.at[wide_at(to)], recv_one.at[c, t - 1])),
                (lambda: (part.at[narrow_at(to)], recv_two.at[c, t - 1])),
                (lambda: (full.at[narrow_at(me_out)],) * 2),
                (lambda: (full.at[wide_at(me_in)],) * 2),
            )[stage]()
            return pltpu.make_async_remote_copy(
                src_ref=source, dst_ref=target,
                send_sem=sends.at[c, stage, t - 1], recv_sem=recvs.at[c, stage, t - 1],
                device_id=device, device_id_type=MESH,
            )

        def copies(stage):
            return [copy(stage, t) for t in range(1, inner if stage in (0, 3) else outer)]

        def start(stage):
            for one in copies(stage):
                one.start()

        def step(stage):
            for one in copies(stage):
                one.wait_recv()
            if stage == 0:
                for one in copies(stage):
                    one.wait_send()
                value = part[wide_at(me_in), :]
                for t in range(inner - 1):
                    value = value + recv_one[c, t]
                part[wide_at(me_in), :] = value
            if stage == 1:
                value = part[narrow_at(me_out), :]
                for t in range(outer - 1):
                    value = value + recv_two[c, t]
                full[narrow_at(me_out), :] = value
            if stage < 3:
                start(stage + 1)

        def drain():
            for stage in range(1, 4):
                for one in copies(stage):
                    one.wait_send()

        return start, step, drain

    (start_a, step_a, drain_a), (start_b, step_b, drain_b) = bulk(0), bulk(1)
    start_a(0)
    start_b(0)

    for t in range(1, inner):
        gram_scatter(t).wait_recv()
    value = part[own_piece, :]
    for t in range(inner - 1):
        value = value + gram_one[t]
    gram_two[me_out] = value
    for t in range(1, outer):
        gram_exchange(t).start()
    for t in range(1, inner):
        gram_scatter(t).wait_send()
    for t in range(1, outer):
        gram_exchange(t).wait_recv()
    value = gram_two[0]
    for o in range(1, outer):
        value = value + gram_two[o]
    gram_own[own_piece, :] = value
    for t in range(1, inner):
        gram_gather(t).start()
    step_a(0)
    for t in range(1, inner):
        gram_gather(t).wait_recv()

    def own_gram(which):
        gram[which] = gram_own[...]

    gram_start, gram_finish, gram_drain = share(
        gram_own, lambda which: gram.at[which], swap_send, swap_recv, own_gram
    )
    gram_start()
    results = []
    if first > 0:
        head = s_ref.at[pl.ds(0, joint)]
        results.append(pltpu.make_async_copy(gram_own, head, out_sem.at[2]))
        results[-1].start()
    step_b(0)
    gram_finish()
    work[:, :PANEL] = gram[0] / total_rows
    work[:, PANEL:joint] = gram[1] / total_rows
    row = lax.broadcasted_iota(jnp.int32, (joint, joint), 0)
    lane = lax.broadcasted_iota(jnp.int32, (joint, joint), 1)
    work[:, joint:] = jnp.where(row == lane, 1.0, 0.0).astype(F32)

    pending = [
        functools.partial(step, stage) for stage in range(1, 4) for step in (step_a, step_b)
    ]
    for at in range(0, joint, BLOCK):
        factor_step(work, at)
        for _ in range(min(2, len(pending) - 2)):
            pending.pop(0)()
    linv_ref[...] = work[:, joint:]
    for step in pending[:-2]:
        step()
    for c, step in enumerate((step_a, step_b)):
        step(3)
        rows = pl.ds(first + c * chunk, chunk)
        results.append(pltpu.make_async_copy(full.at[rows], s_ref.at[rows], out_sem.at[c]))
        results[-1].start()
    points_drain()
    gram_drain()
    for t in range(1, outer):
        gram_exchange(t).wait_send()
    for t in range(1, inner):
        gram_gather(t).wait_send()
    drain_a()
    drain_b()
    for result in results:
        result.wait()


def reduced(descriptors, points, n_rows, n_cols):
    rows, width = descriptors.shape
    cols = points.shape[0]
    joint = 2 * PANEL
    inner = 4 if n_rows % 4 == 0 else 1
    outer = n_rows // inner
    flat = cols // PANEL * joint
    first = joint if (flat - joint) % (16 * n_rows) == 0 else 0
    chunk = (flat - first) // 2
    most = max(inner, outer, 2) - 1
    vmem = pl.BlockSpec(memory_space=pltpu.VMEM)
    dma = pltpu.SemaphoreType.DMA
    return pl.pallas_call(
        functools.partial(reduce_kernel, n_rows, n_cols, inner, float(rows * n_rows)),
        out_shape=(
            jax.ShapeDtypeStruct((joint, width), BF16),
            jax.ShapeDtypeStruct((flat, PANEL), F32),
            jax.ShapeDtypeStruct((joint, joint), F32),
        ),
        in_specs=[pl.BlockSpec(memory_space=pltpu.HBM)] * 2,
        out_specs=(vmem, pl.BlockSpec(memory_space=pl.ANY), vmem),
        scratch_shapes=[
            pltpu.VMEM((rows, width), BF16),
            pltpu.VMEM((cols, width), BF16),
            pltpu.VMEM((joint, width), BF16),
            pltpu.VMEM((rows, cols), BF16),
            pltpu.VMEM((rows, cols), BF16),
            pltpu.VMEM((flat, PANEL), F32),
            pltpu.VMEM((flat, PANEL), F32),
            pltpu.VMEM((2, inner - 1, chunk // inner, PANEL), F32),
            pltpu.VMEM((2, outer - 1, chunk // n_rows, PANEL), F32),
            pltpu.VMEM((inner - 1, joint // inner, PANEL), F32),
            pltpu.VMEM((outer, joint // inner, PANEL), F32),
            pltpu.VMEM((joint, PANEL), F32),
            pltpu.VMEM((2, joint, PANEL), F32),
            pltpu.VMEM((joint, 2 * joint), F32),
            dma((2, n_cols - 1)),
            dma((2,)),
            dma((2, 4, most)),
            dma((2, 4, most)),
            dma((3, most)),
            dma((3, most)),
            dma((2, n_cols - 1)),
            dma((2,)),
            dma((3,)),
            dma((2,)),
        ],
        compiler_params=pltpu.CompilerParams(
            collective_id=0, has_side_effects=True, vmem_limit_bytes=60 * 1024 * 1024
        ),
        name="gram_and_products",
    )(descriptors, points)


def finish_kernel(
    total_rows, d_ref, p_ref, pp_ref, s_ref, linv_ref, q_ref, r_ref, t_ref, r_high, r_low
):
    joint = 2 * PANEL

    @pl.when(pl.program_id(0) == 0)
    def _():
        for block in range(r_ref.shape[1] // joint):
            cols = slice(block * joint, (block + 1) * joint)
            at = block * 2 * joint
            halves = (s_ref[at : at + joint, :], s_ref[at + joint : at + 2 * joint, :])
            sums = jnp.concatenate(halves, axis=1)
            value = dot_nn(linv_ref[...], sums, HIGHEST) / total_rows
            r_ref[:, cols] = value
            r_high[:, cols], r_low[:, cols] = split(value)

    dots = dot_nt(d_ref[...], pp_ref[...])
    q = dot_nt(dots * dots, linv_ref[...], HIGHEST)
    q_ref[...] = q
    q_high, q_low = split(q)
    for block in range(r_ref.shape[1] // joint):
        cols = slice(block * joint, (block + 1) * joint)
        dots = dot_nt(d_ref[...], p_ref[cols, :])
        change = three_pass(q_high, q_low, r_high[:, cols], r_low[:, cols])
        t_ref[:, cols] = (dots * dots - change).astype(BF16)


def finished(descriptors, points, panel_points, sums, inverse, total_rows):
    rows, width = descriptors.shape
    cols = points.shape[0]
    joint = 2 * PANEL
    tile = 256
    whole = lambda shape: pl.BlockSpec(shape, lambda i: (0, 0))
    tiled = lambda lanes: pl.BlockSpec((tile, lanes), lambda i: (i, 0))
    return pl.pallas_call(
        functools.partial(finish_kernel, total_rows),
        out_shape=(
            jax.ShapeDtypeStruct((rows, joint), F32),
            jax.ShapeDtypeStruct((joint, cols), F32),
            jax.ShapeDtypeStruct((rows, cols), BF16),
        ),
        grid=(rows // tile,),
        in_specs=[
            tiled(width),
            whole((cols, width)),
            whole((joint, width)),
            whole(sums.shape),
            whole((joint, joint)),
        ],
        out_specs=(tiled(joint), whole((joint, cols)), tiled(cols)),
        scratch_shapes=[pltpu.VMEM((joint, cols), BF16), pltpu.VMEM((joint, cols), BF16)],
        compiler_params=pltpu.CompilerParams(vmem_limit_bytes=60 * 1024 * 1024),
        name="factors_and_remainder",
    )(descriptors, points, panel_points, sums, inverse)


def solution(mesh):
    n_rows, n_cols = mesh.shape["rows"], mesh.shape["cols"]

    def on_device(descriptors, sparse_points):
        panel_points, sums, inverse = reduced(descriptors, sparse_points, n_rows, n_cols)
        total_rows = float(descriptors.shape[0] * n_rows)
        return finished(descriptors, sparse_points, panel_points, sums, inverse, total_rows)

    in_specs = (P("rows", None), P("cols", None))
    out_specs = (P("rows", None), P(None, "cols"), P("rows", "cols"))
    return jax.shard_map(
        on_device, mesh=mesh, in_specs=in_specs, out_specs=out_specs, check_vma=False
    )
```
